32 devices in a mesh: row: 8 (over z, y), col: 4 (over x, core).
Axes of the slice: x: 2, y: 2, z: 4, core: 2. Of those that a mesh axis runs over, the one named last changes fastest.
Arguments:
- epoch_a: bfloat16 [32, 512, 2048], P(None, 'row', 'col'), may hold values from -6 to 6
- epoch_b: bfloat16 [32, 512, 2048], P(None, 'row', 'col'), may hold values from -6 to 6
- sources: int32 [3, 4, 64, 1], replicated, may hold values from 0 to 7; in each aligned block of 8 rows (0 to 7, 8 to 15, ..., all dimensions but the last counted through in order) at most 2 rows name the same one
Outputs:
- volume_fine: bfloat16 [81, 512, 2048], P(None, 'row', 'col')
- volume_mid: bfloat16 [81, 256, 1024], P(None, 'row', 'col')
- volume_coarse: bfloat16 [81, 128, 512], P(None, 'row', 'col')
The draws below stay inside these ranges and needn't reach their ends.
Inputs may be any that keep to these rules, and one draw needn't show every extreme that they name: `sources`: among the 8 row-blocks of one tile row at one level and one column tile, at most 2 name the same tile row, and 2 is reached in some of them.
All inputs are finite; a program needn't handle non-finite values.
Results may differ from the reference program's by a relative error of at most 0.0063.
Values may be sent and summed in bfloat16 or wider, within the bound.
A program may use at most 704 MiB of HBM per device.

```python
import math
import jax
import jax.numpy as jnp
import numpy as np
from jax import lax

C = 32
LEVELS = 3
CAP = 2
TH = 64
TW = 512
NB = 8
H = 512
W = 2048
N_ROW = 8
N_COL = 4


def shard_levels(rng, extent, shards, least, largest):
    def one(axis_at, blocks):
        steps = jax.random.uniform(jax.random.fold_in(jax.random.fold_in(rng, 6), axis_at), (blocks,), jnp.float32, least / len(shards), largest / len(shards))
        return jnp.repeat(jnp.exp(steps), extent[axis_at] // blocks).reshape((-1,) + (1,) * (len(extent) - axis_at - 1))

    factor_of = one(*shards[0])
    for cut in shards[1:]:
        factor_of = factor_of * one(*cut)
    return factor_of


def routed_block(key, own, number, rows, amount, top, reach, slope):
    ranking = jax.random.permutation(key, amount)
    crowded, ordinary = shares(amount, rows * top, reach, slope, True), shares(amount, rows * top, reach, slope, False)
    places = jnp.arange(amount)

    def named(tallies, turn):
        used = int((tallies > 0).sum())
        fixed = max(1, used // 4)
        moved = fixed + (places - fixed + turn * (used - fixed)) % max(1, amount - fixed)
        return jnp.zeros((amount,), jnp.int32).at[ranking[jnp.where(places < fixed, places, moved)]].set(jnp.asarray(tallies, jnp.int32))

    tallies = jnp.where(number % 4 == 0, named(crowded, number // 4), named(ordinary, number - number // 4 - 1))
    mixed = jax.random.permutation(jax.random.fold_in(own, 3), amount)
    source_of, receiver = mixed[0:amount // 2 * 2:2], mixed[1:amount // 2 * 2:2]
    margin = jnp.minimum(tallies[source_of] - 1, reach - tallies[receiver]) // 2
    margin = jnp.where((source_of == ranking[0]) | (receiver == ranking[0]) | (tallies[receiver] == 0), 0, jnp.maximum(margin, 0))
    moved = jax.random.randint(jax.random.fold_in(own, 4), (amount // 2,), 0, 1 << 20) % (margin + 1)
    tallies = tallies.at[source_of].add(-moved).at[receiver].add(moved)
    items = jnp.searchsorted(jnp.cumsum(tallies), jnp.arange(rows * top), side="right").astype(jnp.int32)
    listing = items.reshape(top, rows).T
    listing = listing[jax.random.permutation(jax.random.fold_in(own, 1), rows)]
    turn = jax.random.randint(jax.random.fold_in(own, 2), (rows, 1), 0, top)
    return jnp.take_along_axis(listing, (jnp.arange(top)[None, :] + turn) % top, axis=1)


def shares(amount, total, bound, skew, full):
    weights = [(1 << 20) // math.isqrt(standing ** skew) + 1 for standing in range(1, amount + 1)]
    largest = bound if full else min(bound, max(-(-total // amount), total * weights[0] // sum(weights)))
    least = 1 if total - largest >= amount - 1 else 0
    holding, spare = [largest] + [least] * (amount - 1), total - largest - least * (amount - 1)
    while spare > 0:
        candidates = [i for i in range(1, amount) if holding[i] < largest] or [i for i in range(1, amount) if holding[i] < bound]
        whole, budget = sum([weights[i] for i in candidates]), spare
        for i in candidates:
            extra = min(bound - holding[i], max(1, budget * weights[i] // whole), spare)
            holding[i] = holding[i] + extra
            spare = spare - extra
    return np.array(holding)


def scatter_about(key, dims, spread, reach, pieces=(), kind=jnp.bfloat16):
    values = jax.random.normal(key, dims, jnp.float32) * spread
    if len(pieces) > 0:
        values = shard_levels(key, dims, pieces, -0.22, 0.18) * values
    return jnp.clip(values, min=-reach, max=reach).astype(kind)


def setup_inputs(seed: int = 0) -> dict:
    key_of = jax.random.split(jax.random.key(seed), 4)
    epoch_a = scatter_about(key_of[0], (C, H, W), 1.0, 6.0, ((1, 8), (2, 4)))
    epoch_b = scatter_about(key_of[1], (C, H, W), 1.0, 6.0, ((1, 8), (2, 4)))
    sources_keys = jax.random.split(jax.random.fold_in(key_of[2], 1), LEVELS * N_COL * (N_ROW * NB) // NB)
    sources_turns = jax.random.permutation(jax.random.fold_in(key_of[2], 3), LEVELS * N_COL * (N_ROW * NB) // NB)
    sources = jax.vmap(lambda own, number: routed_block(jax.random.fold_in(key_of[2], 2), own, number, NB, N_ROW, 1, CAP, 2))(sources_keys, sources_turns).reshape((LEVELS, N_COL, N_ROW * NB, 1))
    return {"epoch_a": epoch_a, "epoch_b": epoch_b, "sources": sources}


GAUSS_TAPS = (1.0, 4.0, 6.0, 4.0, 1.0)
TAP_ENERGY = 70.0 ** 0.5
WINDOW_RIM = 4


def reduce_resolution(padded_image, edge_margin, output_rows, output_columns):
    row_pass = None
    for tap_index in range(5):
        first_row = edge_margin - 2 + tap_index
        shifted = padded_image[..., first_row:first_row + 2 * output_rows:2, :].astype(jnp.float32) * (GAUSS_TAPS[tap_index] / TAP_ENERGY)
        row_pass = shifted if row_pass is None else row_pass + shifted
    result = None
    for tap_index in range(5):
        first_col = edge_margin - 2 + tap_index
        shifted = row_pass[..., first_col:first_col + 2 * output_columns:2] * (GAUSS_TAPS[tap_index] / TAP_ENERGY)
        result = shifted if result is None else result + shifted
    return result.astype(jnp.bfloat16)


def correlate(features, windows):
    height = features.shape[-2]
    breadth = features.shape[-1]
    scaling = features.shape[0] ** -0.5
    anchor = features.astype(jnp.float32)
    planes = []
    for row_offset in range(2 * WINDOW_RIM + 1):
        for col_offset in range(2 * WINDOW_RIM + 1):
            moving = windows[..., row_offset:row_offset + height, col_offset:col_offset + breadth].astype(jnp.float32)
            planes.append(jnp.sum(anchor * moving, axis=0) * scaling)
    return jnp.stack(planes).astype(jnp.bfloat16)


def reference(epoch_a, epoch_b, sources):
    epoch_couple = jnp.stack((epoch_a, epoch_b))
    volumes = []
    for level_index in range(LEVELS):
        patch_rows = TH // 2 ** level_index
        patch_columns = TW // 2 ** level_index
        block_rows = patch_rows // NB
        complete_rows = patch_rows * N_ROW
        complete_columns = patch_columns * N_COL
        searched = jnp.pad(epoch_couple[1], ((0, 0), (WINDOW_RIM, WINDOW_RIM), (WINDOW_RIM, WINDOW_RIM)))
        earlier = epoch_couple[0]
        level_table = sources[level_index]
        block_ids = jnp.arange(N_ROW * NB, dtype=jnp.int32)
        lines = jnp.arange(block_rows + 2 * WINDOW_RIM, dtype=jnp.int32)

        def one_column(column, searched=searched, earlier=earlier, level_table=level_table,
                       patch_rows=patch_rows, patch_columns=patch_columns, block_rows=block_rows,
                       complete_rows=complete_rows, block_ids=block_ids, lines=lines):
            root = (column * patch_columns).astype(jnp.int32)
            strip = lax.dynamic_slice_in_dim(searched, root, patch_columns + 2 * WINDOW_RIM, 2)
            anchors = lax.dynamic_slice_in_dim(earlier, root, patch_columns, 2)
            tiles_from = lax.dynamic_index_in_dim(level_table, column, 0, keepdims=False)[:, 0].astype(jnp.int32)
            row_index = tiles_from[:, None] * patch_rows + (block_ids % NB)[:, None] * block_rows + lines[None, :]
            windows = strip[:, row_index, :]
            features = anchors.reshape(C, N_ROW * NB, block_rows, patch_columns)
            return correlate(features, windows).reshape(81, complete_rows, patch_columns)

        stacked = lax.map(one_column, jnp.arange(N_COL, dtype=jnp.int32))
        volumes.append(jnp.moveaxis(stacked, 0, 2).reshape(81, complete_rows, complete_columns))
        if level_index + 1 < LEVELS:
            bordered_image = jnp.pad(epoch_couple, ((0, 0), (0, 0), (2, 2), (2, 2)))
            epoch_couple = reduce_resolution(bordered_image, 2, complete_rows // 2, complete_columns // 2)
    return (volumes[0], volumes[1], volumes[2])
```

```python
import jax
import jax.numpy as jnp
import numpy as np
from jax import lax
from jax.experimental import pallas as pl
from jax.experimental.pallas import tpu as pltpu
from jax.sharding import PartitionSpec as P

LEVELS = 3
GAUSS_TAPS = (1.0, 4.0, 6.0, 4.0, 1.0)
TAP_ENERGY = 70.0**0.5
WINDOW_RIM = 4
SPAN = 2 * WINDOW_RIM + 1
LANES = 128
SUBLANES = 8


def padded(x, sides, width):
    for axis, dim in sides:
        count, length = (lax.axis_size(axis), x.shape[dim])
        up = [(i, (i + 1) % count) for i in range(count - 1)]
        down = [(j, i) for i, j in up]
        last = lax.slice_in_dim(x, length - width, length, axis=dim)
        initial = lax.slice_in_dim(x, 0, width, axis=dim)
        before = lax.ppermute(last, axis, up)
        after = lax.ppermute(initial, axis, down)
        x = jnp.concatenate([before, x, after], axis=dim)
    return x


def reduce_resolution(padded_image, edge_margin, output_rows, output_columns):
    row_pass = None
    for tap_index in range(5):
        first_row = edge_margin - 2 + tap_index
        shifted = padded_image[..., first_row : first_row + 2 * output_rows : 2, :].astype(
            jnp.float32
        ) * (GAUSS_TAPS[tap_index] / TAP_ENERGY)
        row_pass = shifted if row_pass is None else row_pass + shifted
    band = np.zeros((padded_image.shape[-1], output_columns), np.float32)
    for tap_index in range(5):
        places = np.arange(output_columns)
        band[edge_margin - 2 + tap_index + 2 * places, places] = (
            GAUSS_TAPS[tap_index] / TAP_ENERGY
        )
    result = jnp.einsum(
        "ecrw,wv->ecrv",
        row_pass,
        jnp.asarray(band),
        precision=lax.Precision.HIGHEST,
        preferred_element_type=jnp.float32,
    )
    return result.astype(jnp.bfloat16)


def correlate_kernel(features_ref, windows_ref, out_ref, moved, planes):
    channels, block_rows, block_count, breadth = features_ref.shape
    extent = windows_ref.shape[-1]
    window_rows = windows_ref.shape[1]
    scaling = channels ** (-0.5)
    turn = lax.rem(extent - pl.program_id(0), extent)

    def shift(c, carry):
        flat = windows_ref[c].reshape(window_rows * block_count, extent)
        rolled = pltpu.roll(flat, turn, 1)[:, :breadth]
        moved[c] = rolled.reshape(window_rows, block_count, breadth)
        return carry

    lax.fori_loop(0, channels, shift, 0)
    group = min(block_rows, 4)
    for first in range(0, block_rows, group):
        for top in range(0, block_count, SUBLANES):
            for left in range(0, breadth, LANES):
                rows = slice(top, top + SUBLANES)
                cols = slice(left, left + LANES)

                def step(c, sums, first=first, rows=rows, cols=cols):
                    anchors = [features_ref[c, first + u, rows, cols] for u in range(group)]
                    others = [
                        moved[c, first + r, rows, cols] for r in range(group + SPAN - 1)
                    ]
                    return tuple(
                        sums[u * SPAN + dy] + anchors[u] * others[u + dy]
                        for u in range(group)
                        for dy in range(SPAN)
                    )

                zero = jnp.zeros((SUBLANES, LANES), jnp.float32)
                sums = lax.fori_loop(0, channels, step, (zero,) * (group * SPAN), unroll=8)
                for u in range(group):
                    for dy in range(SPAN):
                        start = top * block_rows + first + u
                        if block_rows == 1:
                            where = pl.ds(start, SUBLANES)
                        else:
                            where = pl.ds(start, SUBLANES, stride=block_rows)
                        planes[left // LANES, dy, where, :] = sums[u * SPAN + dy] * scaling

    for dy in range(SPAN):
        for left in range(0, breadth, LANES):
            out_ref[dy, 0, :, left : left + LANES] = planes[left // LANES, dy].astype(jnp.bfloat16)


def correlate(features, windows):
    channels, block_rows, block_count, breadth = features.shape
    rows = block_rows * block_count
    flops = 2 * SPAN * SPAN * channels * rows * breadth
    volume = pl.pallas_call(
        correlate_kernel,
        grid=(SPAN,),
        out_shape=jax.ShapeDtypeStruct((SPAN, SPAN, rows, breadth), jnp.bfloat16),
        in_specs=[
            pl.BlockSpec(features.shape, lambda i: (0, 0, 0, 0), pipeline_mode=pl.Buffered(1)),
            pl.BlockSpec(windows.shape, lambda i: (0, 0, 0, 0), pipeline_mode=pl.Buffered(1)),
        ],
        out_specs=pl.BlockSpec((SPAN, 1, rows, breadth), lambda i: (0, i, 0, 0)),
        scratch_shapes=[
            pltpu.VMEM(windows.shape[:3] + (breadth,), jnp.float32),
            pltpu.VMEM((breadth // LANES, SPAN, rows, LANES), jnp.float32),
        ],
        compiler_params=pltpu.CompilerParams(vmem_limit_bytes=50 * 1024 * 1024),
        cost_estimate=pl.CostEstimate(
            flops=flops,
            bytes_accessed=4 * (features.size + windows.size) + 2 * SPAN * SPAN * rows * breadth,
            transcendentals=0,
        ),
    )(features, windows)
    return volume.reshape(SPAN * SPAN, rows, breadth)


def level_windows(search, wanted, block_count, block_rows):
    tiles = lax.all_gather(search, "row", axis=0)
    extra = -search.shape[-1] % LANES
    pieces = []
    for k in range(block_count):
        piece = lax.dynamic_slice(
            tiles,
            (wanted[k], 0, k * block_rows, 0),
            (1, search.shape[0], block_rows + 2 * WINDOW_RIM, search.shape[-1]),
        )[0]
        pieces.append(piece.astype(jnp.float32))
    return jnp.pad(jnp.stack(pieces, axis=2), ((0, 0), (0, 0), (0, 0), (0, extra)))


def local(epoch_a, epoch_b, sources):
    row_me = lax.axis_index("row")
    col_me = lax.axis_index("col")
    row_devices = lax.axis_size("row")
    epoch_couple = jnp.stack((epoch_a, epoch_b))
    volumes = []
    for level_index in range(LEVELS):
        _, channels, patch_rows, patch_columns = epoch_couple.shape
        block_rows = patch_rows // row_devices
        column_table = lax.dynamic_index_in_dim(sources[level_index], col_me, 0, keepdims=False)[
            :, 0
        ]
        table = column_table.reshape(row_devices, row_devices)
        wanted = lax.dynamic_index_in_dim(table, row_me, 0, keepdims=False)
        features = jnp.swapaxes(
            epoch_couple[0].reshape(channels, row_devices, block_rows, patch_columns), 1, 2
        ).astype(jnp.float32)
        if level_index + 1 < LEVELS:
            bordered = padded(epoch_couple, (("row", 2), ("col", 3)), WINDOW_RIM)
            search = bordered[1]
            epoch_couple = reduce_resolution(
                bordered, WINDOW_RIM, patch_rows // 2, patch_columns // 2
            )
        else:
            search = padded(epoch_couple[1], (("row", 1), ("col", 2)), WINDOW_RIM)
        windows = level_windows(search, wanted, row_devices, block_rows)
        volumes.append(correlate(features, windows))
    return tuple(volumes)


def solution(mesh):
    return jax.shard_map(
        local,
        mesh=mesh,
        in_specs=(P(None, "row", "col"), P(None, "row", "col"), P()),
        out_specs=(P(None, "row", "col"), P(None, "row", "col"), P(None, "row", "col")),
        check_vma=False,
    )
```
